256 devices in a mesh: fsdp: 64 (over z_lo, y, x), seq: 4 (over z_hi, core).
Axes of the slice: x: 4, y: 4, z: 8 (z_hi: 2, z_lo: 4; z = z_hi * 4 + z_lo), core: 2. Of those that a mesh axis runs over, the one named last changes fastest.
Arguments:
- queries: bfloat16 [64, 768, 2048], P('fsdp', 'seq'), may hold values from -8 to 8, as said below
- keys: bfloat16 [64, 768, 2048], P('fsdp', 'seq'), may hold values from -8 to 8, as said below
- values: bfloat16 [64, 768, 2048], P('fsdp', 'seq'), may hold values from -6 to 6
- out_grad: bfloat16 [64, 768, 4096], P('fsdp', 'seq'), may hold values from -3 to 3
- out_weight: bfloat16 [2048, 4096], P('fsdp', 'seq'), may hold values from -0.125 to 0.125
- time_gate: float32 [32, 4096], replicated, may hold values from -3 to 3
- speaker_gate: float32 [64, 4096], replicated, may hold values from -3 to 3
- time_steps: int32 [64], replicated, may hold values from 0 to 31
- speakers: int32 [64], replicated, may hold values from 0 to 63
- lengths: int32 [64], replicated, may hold values from 384 to 768, as said below
Outputs:
- query_grad: bfloat16 [64, 768, 2048], P('fsdp', 'seq')
- key_grad: bfloat16 [64, 768, 2048], P('fsdp', 'seq')
- value_grad: bfloat16 [64, 768, 2048], P('fsdp', 'seq')
- time_gate_grad: float32 [32, 4096], replicated
- speaker_gate_grad: float32 [64, 4096], replicated
The draws below stay inside these ranges and needn't reach their ends.
Inputs may be any that keep to these rules, and one draw needn't show every extreme that they name: `queries`: queries lie within this range. `keys`: keys lie within this range. `lengths`: some clip has all 768 frames live.
All inputs are finite; a program needn't handle non-finite values.
Results may differ from the reference program's by a relative error of at most 0.038.
Values may be sent and summed in bfloat16 or wider, within the bound.
A program may use at most 128 MiB of HBM per device.

```python
import jax
import jax.numpy as jnp
from jax import lax

D = 4096
HEADS = 16
HEAD_DIM = 128
HD = 2048
FRAMES = 768
CLIPS = 64
TT = 32
SPK = 64
N_SEQ = 4


def draw_keys(key, part):
    key = jax.random.fold_in(key, 11)
    shape = (CLIPS, FRAMES, HEADS * HEAD_DIM)
    vals = jnp.clip(jax.random.normal(key, shape, jnp.float32), -4.0, 4.0)
    return vals.astype(jnp.bfloat16)


def draw_queries(key, part):
    key = jax.random.fold_in(key, 23)
    shape = (CLIPS, FRAMES, HEADS * HEAD_DIM)
    vals = jnp.clip(jax.random.normal(key, shape, jnp.float32), -4.0, 4.0)
    return vals.astype(jnp.bfloat16)


def draw_lengths(key, part):
    key = jax.random.fold_in(key, 5)
    first, second = jax.random.split(key)
    vals = jax.random.randint(first, (CLIPS,), FRAMES // 2, FRAMES + 1)
    chosen = jax.random.randint(second, (), 0, CLIPS)
    return jnp.where(jnp.arange(CLIPS) == chosen, FRAMES, vals).astype(jnp.int32)


def set_ends(array, own_key, low, top_value):
    shape = array.shape
    spot = [jax.random.randint(jax.random.fold_in(own_key, axis), (), 0, shape[axis]) for axis in range(len(shape))]
    array = array.at[tuple(spot)].set(low)
    longest = shape.index(max(shape))
    spot[longest] = (spot[longest] + 1) % shape[longest]
    return array.at[tuple(spot)].set(top_value)


def levels(rng, extent, cuts, smallest, high):
    loudness = 1.0
    for axis_at, blocks in cuts:
        draws = jax.random.uniform(jax.random.fold_in(jax.random.fold_in(rng, 6), axis_at), (blocks,), jnp.float32, smallest / len(cuts), high / len(cuts))
        loudness = loudness * jnp.repeat(jnp.exp(draws), extent[axis_at] // blocks).reshape((-1,) + (1,) * (len(extent) - 1 - axis_at))
    return loudness


def bell_draw(own_key, extent, spread, reach, cuts=(), kind=jnp.bfloat16):
    drawn = spread * jax.random.normal(own_key, extent, jnp.float32)
    if cuts:
        drawn = drawn * levels(own_key, extent, cuts, -0.22, 0.18)
    return jnp.clip(drawn, -reach, reach).astype(kind)


def setup_inputs(seed: int = 0) -> dict:
    arg_keys = jax.random.split(jax.random.key(seed), 11)
    queries = draw_queries(jax.random.fold_in(arg_keys[10], 71), 0)
    keys = draw_keys(jax.random.fold_in(arg_keys[10], 71), 0)
    values = bell_draw(arg_keys[2], (CLIPS, FRAMES, HD), 1.0, 6.0, ((0, 64), (1, 4)))
    out_grad = bell_draw(arg_keys[3], (CLIPS, FRAMES, D), 0.5, 3.0, ((0, 64), (1, 4)))
    out_weight = bell_draw(arg_keys[4], (HD, D), HD ** -0.5, 0.125, ((0, 64), (1, 4)))
    time_gate = bell_draw(arg_keys[5], (TT, D), 0.5, 3.0, (), jnp.float32)
    speaker_gate = bell_draw(arg_keys[6], (SPK, D), 0.5, 3.0, (), jnp.float32)
    time_steps = set_ends(jax.random.randint(arg_keys[7], (CLIPS,), 0, TT), jax.random.fold_in(arg_keys[7], 1), 0, TT - 1).astype(jnp.int32)
    speakers = set_ends(jax.random.randint(arg_keys[8], (CLIPS,), 0, SPK), jax.random.fold_in(arg_keys[8], 1), 0, SPK - 1).astype(jnp.int32)
    lengths = draw_lengths(jax.random.fold_in(arg_keys[10], 71), 0)
    return dict(queries=queries, keys=keys, values=values, out_grad=out_grad, out_weight=out_weight, time_gate=time_gate, speaker_gate=speaker_gate, time_steps=time_steps, speakers=speakers, lengths=lengths)


def to_low(x):
    low = x.astype(jnp.bfloat16)
    low = lax.optimization_barrier(low)
    return low.astype(jnp.float32)


def clip_grads(query, key_in, value, grad_out, out_weight, gate, length):
    frames = query.shape[0]
    scale = HEAD_DIM ** -0.5
    query_h = query.reshape(frames, HEADS, HEAD_DIM).astype(jnp.float32)
    key_h = key_in.reshape(frames, HEADS, HEAD_DIM).astype(jnp.float32)
    value_h = value.reshape(frames, HEADS, HEAD_DIM).astype(jnp.float32)
    live = jnp.arange(frames) < length
    scores = jnp.einsum('qhd,khd->hqk', query_h, key_h) * scale
    scores = jnp.where(live[None, None, :], scores, -1e30)
    top = jnp.max(scores, axis=-1, keepdims=True)
    expo = jnp.exp(scores - top)
    probs = expo / jnp.sum(expo, axis=-1, keepdims=True)
    probs_low = to_low(probs)
    heads_out = jnp.einsum('hqk,khd->qhd', probs_low, value_h).reshape(frames, HD).astype(jnp.bfloat16)
    proj = jnp.dot(heads_out, out_weight, preferred_element_type=jnp.float32)
    gate_grad = jnp.sum(grad_out.astype(jnp.float32) * proj, axis=0)
    scaled = (grad_out.astype(jnp.float32) * gate[None, :]).astype(jnp.bfloat16)
    heads_grad = lax.dot_general(scaled, out_weight, (((1,), (1,)), ((), ())), preferred_element_type=jnp.float32).astype(jnp.bfloat16)
    grad_h = heads_grad.reshape(frames, HEADS, HEAD_DIM).astype(jnp.float32)
    out_h = heads_out.reshape(frames, HEADS, HEAD_DIM).astype(jnp.float32)
    delta = jnp.sum(grad_h * out_h, axis=-1).T
    prob_grad = jnp.einsum('qhd,khd->hqk', grad_h, value_h)
    score_grad = to_low(probs * (prob_grad - delta[:, :, None]))
    query_grad = (jnp.einsum('hqk,khd->qhd', score_grad, key_h) * scale).reshape(frames, HD).astype(jnp.bfloat16)
    block = frames // N_SEQ
    score_blocks = score_grad.reshape(HEADS, N_SEQ, block, frames)
    prob_blocks = probs_low.reshape(HEADS, N_SEQ, block, frames)
    query_blocks = query_h.reshape(N_SEQ, block, HEADS, HEAD_DIM)
    grad_blocks = grad_h.reshape(N_SEQ, block, HEADS, HEAD_DIM)
    key_part = (jnp.einsum('hjqk,jqhd->jkhd', score_blocks, query_blocks) * scale).astype(jnp.bfloat16)
    value_part = jnp.einsum('hjqk,jqhd->jkhd', prob_blocks, grad_blocks).astype(jnp.bfloat16)
    key_grad = jnp.sum(key_part.astype(jnp.float32), axis=0).reshape(frames, HD).astype(jnp.bfloat16)
    value_grad = jnp.sum(value_part.astype(jnp.float32), axis=0).reshape(frames, HD).astype(jnp.bfloat16)
    return query_grad, key_grad, value_grad, gate_grad


def reference(queries, keys, values, out_grad, out_weight, time_gate, speaker_gate, time_steps, speakers, lengths):
    gates = time_gate[time_steps] + speaker_gate[speakers]

    def one_clip(items):
        query, key_in, value, grad_out, gate, length = items
        return clip_grads(query, key_in, value, grad_out, out_weight, gate, length)

    query_grad, key_grad, value_grad, gate_grads = lax.map(one_clip, (queries, keys, values, out_grad, gates, lengths))
    time_hot = (jnp.arange(TT)[:, None] == time_steps[None, :]).astype(jnp.float32)
    speaker_hot = (jnp.arange(SPK)[:, None] == speakers[None, :]).astype(jnp.float32)
    time_gate_grad = jnp.dot(time_hot, gate_grads, precision=lax.Precision.HIGHEST)
    speaker_gate_grad = jnp.dot(speaker_hot, gate_grads, precision=lax.Precision.HIGHEST)
    return (query_grad, key_grad, value_grad, time_gate_grad, speaker_gate_grad)
```

```python
import functools
import math

import jax
import jax.numpy as jnp
from jax import lax
from jax.experimental import pallas as pl
from jax.experimental.pallas import tpu as pltpu
from jax.sharding import PartitionSpec as P

HEAD_DIM = 128
LOCAL_HEADS = 8
HALF = 384
ROWS = 192
FEAT = 1024
D = 4096
TT = 32
SPK = 64
SCALE = HEAD_DIM ** (-0.5)
SCALE2 = SCALE / math.log(2.0)
MESH = pl.DeviceIdType.MESH
BF = jnp.bfloat16
F32 = jnp.float32

NT = (((1,), (1,)), ((), ()))
NN = (((1,), (0,)), ((), ()))
TN = (((0,), (0,)), ((), ()))


def dot(a, b, dims):
    return lax.dot_general(a, b, dims, preferred_element_type=F32)


def kernel(
    ts_ref, sp_ref, ln_ref,
    q_in, k_in, v_in, g_in, w_in, tg_in, sg_in,
    dq_out, dk_out, dv_out, tt_out, st_out,
    qb, kb, vb, db, gb, sb, wb, ob, dqv, dkv, dvv, dka, dva, stats,
    gp, gx, zb, gat, ttv, stv, tgv, sgv,
    loc, ps, pr, wzs, wzr, ws, wr, zs, zr, ds_s, ds_r, g1, gzs, gzr, gxs, gxr, ol, os, orc,
):
    fs = lax.axis_index("fsdp")
    sq = lax.axis_index("seq")
    x = lax.rem(fs, 4)
    y = lax.rem(lax.div(fs, 4), 4)
    zl = lax.div(fs, 16)
    zh = lax.div(sq, 2)
    c = lax.rem(sq, 2)
    z = zh * 4 + zl
    oc = 1 - c

    def dev(dz=0, dy=0, dx=0, fc=0):
        z2 = lax.rem(z + dz, 8)
        y2 = lax.rem(y + dy, 4)
        x2 = lax.rem(x + dx, 4)
        c2 = oc if fc else c
        return (lax.rem(z2, 4) * 16 + y2 * 4 + x2, lax.div(z2, 4) * 2 + c2)

    def remote(src, dst, ss, rs, to):
        return pltpu.make_async_remote_copy(
            src_ref=src, dst_ref=dst, send_sem=ss, recv_sem=rs, device_id=to, device_id_type=MESH
        )

    partner = dev(fc=1)
    anti = dev(dz=4)

    bar = pltpu.get_barrier_semaphore()
    peers = [partner]
    peers += [dev(dz=d) for d in range(1, 8)]
    peers += [dev(dx=d) for d in range(1, 4)]
    peers += [dev(dy=d) for d in range(1, 4)]
    for p in peers:
        pl.semaphore_signal(bar, inc=1, device_id=p, device_id_type=MESH)
    pl.semaphore_wait(bar, len(peers))

    my_rows = pl.ds(pl.multiple_of(c * ROWS, 64), ROWS)
    ot_rows = pl.ds(pl.multiple_of(oc * ROWS, 64), ROWS)
    my_cols = pl.ds(pl.multiple_of(c * FEAT, FEAT), FEAT)
    ot_cols = pl.ds(pl.multiple_of(oc * FEAT, FEAT), FEAT)

    ch = lax.div(zl, 2)
    wt = lax.rem(zl, 2)
    wrow = pl.ds(pl.multiple_of(wt * 512 + y * 128 + x * 32, 32), 32)
    wcol = pl.ds(pl.multiple_of(sq * 1024, 1024), 1024)
    w_own = pltpu.make_async_copy(w_in, wb.at[wrow, wcol], loc.at[4])
    w_pair = remote(w_in, wb.at[wrow, wcol], ps.at[4], pr.at[4], partner)
    pl.when(c == ch)(w_own.start)
    pl.when(c != ch)(w_pair.start)

    pair = []
    for n, (src, dst) in enumerate(((k_in, kb), (v_in, vb), (q_in, qb))):
        pair.append((
            pltpu.make_async_copy(src.at[:, my_cols], dst.at[my_rows, :], loc.at[n]),
            remote(src.at[:, ot_cols], dst.at[my_rows, :], ps.at[n], pr.at[n], partner),
            remote(src.at[:, ot_cols], dst.at[ot_rows, :], ps.at[n], pr.at[n], partner),
        ))
    pair.append((
        pltpu.make_async_copy(g_in, gb.at[my_rows, :], loc.at[3]),
        remote(g_in, gb.at[my_rows, :], ps.at[3], pr.at[3], partner),
        remote(g_in, gb.at[ot_rows, :], ps.at[3], pr.at[3], partner),
    ))
    for a, b, _ in pair:
        b.start()
        a.start()
    tg_copy = pltpu.make_async_copy(tg_in, tgv, loc.at[5])
    sg_copy = pltpu.make_async_copy(sg_in, sgv, loc.at[6])
    tg_copy.start()
    sg_copy.start()

    wz_src = wb.at[wrow, pl.ds(pl.multiple_of(zh * 2048, 2048), 2048)]
    wz_out = [remote(wz_src, wz_src, wzs.at[d], wzr.at[wt * 2 + zh], dev(dz=d)) for d in range(1, 8)]

    @pl.when(c == ch)
    def _():
        w_own.wait()
        remote(
            w_in, wb.at[wrow, pl.ds(pl.multiple_of((zh * 2 + oc) * 1024, 1024), 1024)],
            ps.at[4], pr.at[4], partner,
        ).wait_recv()
        for cp in wz_out:
            cp.start()

    def head(j):
        return pl.ds(pl.multiple_of(j * HEAD_DIM, HEAD_DIM), HEAD_DIM)

    own = pl.ds(0, HALF)
    other = pl.ds(HALF, HALF)

    def zcopy(n, j):
        buf = (kb, vb, qb, db)[n]
        return remote(
            buf.at[own, head(j)], buf.at[other, head(j)], zs.at[n, j], zr.at[n, j], anti
        )

    def pair_wait(n):
        a, _, r = pair[n]
        a.wait()
        r.wait_recv()

    pair_wait(0)
    pair_wait(1)

    @pl.loop(0, LOCAL_HEADS)
    def _(j):
        zcopy(0, j).start()
        zcopy(1, j).start()

    pair_wait(2)

    @pl.loop(0, LOCAL_HEADS)
    def _(j):
        zcopy(2, j).start()

    tg_copy.wait()
    sg_copy.wait()
    gate = tgv[pl.ds(ts_ref[fs], 1), :] + sgv[pl.ds(sp_ref[fs], 1), :]
    pair_wait(3)
    for blk in range(8):
        cols = slice(blk * 512, (blk + 1) * 512)
        sb[:, cols] = (gb[:, cols].astype(F32) * gate[:, cols]).astype(BF)

    for t in range(2):
        for h in range(2):
            reg = wb.at[
                pl.ds(pl.multiple_of(t * 512 + y * 128 + x * 32, 32), 32),
                pl.ds(h * 2048, 2048),
            ]
            mine = jnp.logical_and(c == ch, jnp.logical_and(wt == t, zh == h))
            cp = remote(reg, reg, wzs.at[1], wzr.at[t * 2 + h], partner)
            pl.when(jnp.logical_not(mine))(cp.wait_recv)

    def unit(t, d1):
        if t == 0:
            r = y * 128 + lax.rem(x + 4 - d1, 4) * 32
        else:
            r = 512 + lax.rem(y + 4 - d1, 4) * 128 + x * 32
        return wb.at[pl.ds(pl.multiple_of(r, 32), 32), :]

    def axis_dev(axis, d):
        return dev(dx=d) if axis == 0 else dev(dy=d)

    def w1(t, d):
        return remote(unit(t, 0), unit(t, 0), ws.at[t, d, 0], wr.at[t, d, 0], axis_dev(t, d))

    def w2(t, d1, e):
        u = unit(t, d1)
        return remote(u, u, ws.at[t, d1, e], wr.at[t, d1, e], axis_dev(1 - t, e))

    for d in (1, 3, 2):
        for t in range(2):
            w1(t, d).start()
    for e in (1, 3, 2):
        for t in range(2):
            w2(t, 0, e).start()

    def w_forward():
        for d1 in (1, 3, 2):
            for t in range(2):
                u = unit(t, d1)
                remote(u, u, ws.at[t, d1, 0], wr.at[t, d1, 0], partner).wait_recv()
                for e in (1, 3, 2):
                    w2(t, d1, e).start()

    def w_finish():
        for d1 in range(4):
            for t in range(2):
                for e in range(1, 4):
                    if t == 0:
                        r = lax.rem(y + 4 - e, 4) * 128 + lax.rem(x + 4 - d1, 4) * 32
                    else:
                        r = 512 + lax.rem(y + 4 - d1, 4) * 128 + lax.rem(x + 4 - e, 4) * 32
                    u = wb.at[pl.ds(pl.multiple_of(r, 32), 32), :]
                    remote(u, u, ws.at[t, d1, e], wr.at[t, d1, e], partner).wait_recv()

    length = ln_ref[fs]
    key_pos = lax.broadcasted_iota(jnp.int32, (2 * HALF, 1), 0)
    frame = jnp.where(key_pos < HALF, zh * HALF + key_pos, (1 - zh) * HALF + key_pos - HALF)
    live = frame < length

    @pl.loop(0, LOCAL_HEADS)
    def _(j):
        pl.when(j == 1)(w_forward)
        zcopy(0, j).wait_recv()
        zcopy(1, j).wait_recv()
        s = dot(kb[:, head(j)], qb[own, head(j)], NT) * SCALE2
        s = jnp.where(live, s, -1e30)
        top = jnp.max(s, axis=0, keepdims=True)
        e = jnp.exp2(s - top)
        tot = jnp.sum(e, axis=0, keepdims=True)
        p = (e * (1.0 / tot)).astype(BF)
        ob[:, head(j)] = dot(p, vb[:, head(j)], TN).astype(BF)
        stats[0, j, 0:1, :] = top + jnp.log2(tot)

    w_finish()
    ones = jnp.ones((8, HEAD_DIM), F32)

    @pl.loop(0, LOCAL_HEADS // 2)
    def _(i):
        two = pl.ds(pl.multiple_of(i * 256, 256), 256)
        db[own, two] = dot(sb[...], wb[two, :], NT).astype(BF)
        for k in range(2):
            j = 2 * i + k
            prod = db[own, head(j)].astype(F32) * ob[:, head(j)].astype(F32)
            delta = lax.dot_general(
                ones, prod, NT, preferred_element_type=F32, precision=lax.Precision.HIGHEST
            )
            stats[0, j, 1:2, :] = delta[0:1, :]
            zcopy(3, j).start()
            remote(stats.at[0, j], stats.at[1, j], ds_s.at[j], ds_r.at[j], anti).start()

    @pl.loop(0, 16)
    def _(i):
        cols = pl.ds(pl.multiple_of(i * 256, 256), 256)
        proj = dot(ob[...], wb[:, cols], NN)
        part = jnp.sum(proj * gb[:, cols].astype(F32), axis=0, keepdims=True)
        gp[lax.div(i, 8), pl.ds(lax.rem(i, 8), 1), :] = part

    g1_copy = remote(gp.at[oc], gx, g1.at[0], g1.at[1], partner)
    g1_copy.start()

    gz_out = [remote(zb.at[z], zb.at[z], gzs.at[d], gzr.at[z], dev(dz=d)) for d in range(1, 8)]
    gx_src = gat.at[:, y, x]
    gx_out = [remote(gx_src, gx_src, gxs.at[0, d], gxr.at[0, d], dev(dx=d)) for d in range(1, 4)]
    gy_src = gat.at[:, y]
    gy_out = [remote(gy_src, gy_src, gxs.at[1, d], gxr.at[1, d], dev(dy=d)) for d in range(1, 4)]

    def gate_z():
        g1_copy.wait()
        zb[z] = gp[c] + gx[...]
        for cp in gz_out:
            cp.start()

    def gate_x():
        for d in range(1, 8):
            zz = lax.rem(z + d, 8)
            remote(zb.at[zz], zb.at[zz], gzs.at[d], gzr.at[zz], partner).wait_recv()
        for k in range(4):
            gat[k, y, x] = zb[k] + zb[k + 4]
        for cp in gx_out:
            cp.start()

    def gate_y():
        for d in range(1, 4):
            r = gat.at[:, y, lax.rem(x + 4 - d, 4)]
            remote(r, r, gxs.at[0, d], gxr.at[0, d], partner).wait_recv()
        for cp in gy_out:
            cp.start()

    my_tab = pl.ds(pl.multiple_of(c * 2048, 2048), 2048)
    tab = []
    for n, (src, dst) in enumerate(((ttv, tt_out), (stv, st_out))):
        tab.append(pltpu.make_async_copy(src, dst.at[:, my_tab], ol.at[3 + n]))
        tab.append(remote(src, dst.at[:, my_tab], os.at[3 + n], orc.at[3 + n], partner))

    def gate_tables():
        for d in range(1, 4):
            r = gat.at[:, lax.rem(y + 4 - d, 4)]
            remote(r, r, gxs.at[1, d], gxr.at[1, d], partner).wait_recv()
        tcol = jnp.concatenate([jnp.full((1, 1), ts_ref[k], jnp.int32) for k in range(64)], axis=1)
        scol = jnp.concatenate([jnp.full((1, 1), sp_ref[k], jnp.int32) for k in range(64)], axis=1)
        hot_t = (lax.broadcasted_iota(jnp.int32, (TT, 64), 0) == tcol).astype(F32)
        hot_s = (lax.broadcasted_iota(jnp.int32, (SPK, 64), 0) == scol).astype(F32)
        for r in range(8):
            rows = gat[:, :, :, r, :].reshape(64, 256)
            cols = slice(r * 256, (r + 1) * 256)
            for hot, dst in ((hot_t, ttv), (hot_s, stv)):
                dst[:, cols] = lax.dot_general(
                    hot, rows, NN, preferred_element_type=F32, precision=lax.Precision.HIGHEST
                )
        for cp in tab:
            cp.start()

    outs = ((dqv, dq_out), (dkv, dk_out), (dvv, dv_out))

    def out_copies(n, j):
        src, dst = outs[n]
        to = dst.at[:, pl.ds(pl.multiple_of(c * FEAT + j * HEAD_DIM, HEAD_DIM), HEAD_DIM)]
        return (
            pltpu.make_async_copy(src.at[my_rows, head(j)], to, ol.at[n]),
            remote(src.at[ot_rows, head(j)], to, os.at[n], orc.at[n], partner),
        )

    @pl.loop(0, LOCAL_HEADS)
    def _(j):
        q = qb[own, head(j)]
        k = kb[:, head(j)]
        do = db[own, head(j)]
        s = jnp.where(live, dot(k, q, NT) * SCALE2, -1e30)
        p = jnp.exp2(s - stats[0, j, 0:1, :])
        dp = dot(vb[:, head(j)], do, NT)
        ds = (p * (dp - stats[0, j, 1:2, :])).astype(BF)
        dqv[:, head(j)] = (dot(ds, k, TN) * SCALE).astype(BF)
        dka[:, head(j)] = dot(ds[:HALF], q, NN)
        dva[:, head(j)] = dot(p[:HALF].astype(BF), do, NN)
        for cp in out_copies(0, j):
            cp.start()
        pl.when(j == 0)(gate_z)
        pl.when(j == 3)(gate_x)
        pl.when(j == 5)(gate_y)

    gate_tables()

    @pl.loop(0, LOCAL_HEADS)
    def _(j):
        zcopy(2, j).wait_recv()
        zcopy(3, j).wait_recv()
        remote(stats.at[0, j], stats.at[1, j], ds_s.at[j], ds_r.at[j], anti).wait_recv()
        q = qb[other, head(j)]
        do = db[other, head(j)]
        s = jnp.where(live[:HALF], dot(kb[own, head(j)], q, NT) * SCALE2, -1e30)
        p = jnp.exp2(s - stats[1, j, 0:1, :])
        dp = dot(vb[own, head(j)], do, NT)
        ds = (p * (dp - stats[1, j, 1:2, :])).astype(BF)
        dkv[:, head(j)] = ((dka[:, head(j)] + dot(ds, q, NN)) * SCALE).astype(BF)
        dvv[:, head(j)] = (dva[:, head(j)] + dot(p.astype(BF), do, NN)).astype(BF)
        for n in (1, 2):
            for cp in out_copies(n, j):
                cp.start()

    for _, b, _ in pair:
        b.wait_send()
    pl.when(c != ch)(w_pair.wait_send)

    @pl.when(c == ch)
    def _():
        for cp in wz_out:
            cp.wait_send()

    for t in range(2):
        for d in range(1, 4):
            w1(t, d).wait_send()
        for d1 in range(4):
            for e in range(1, 4):
                w2(t, d1, e).wait_send()

    @pl.loop(0, LOCAL_HEADS)
    def _(j):
        for n in range(4):
            zcopy(n, j).wait_send()
        remote(stats.at[0, j], stats.at[1, j], ds_s.at[j], ds_r.at[j], anti).wait_send()

    for cp in gz_out + gx_out + gy_out:
        cp.wait_send()
    for n, (src, dst) in enumerate(outs):
        pltpu.make_async_copy(src.at[my_rows, :], dst.at[:, my_cols], ol.at[n]).wait()
        whole = remote(src.at[ot_rows, :], dst.at[:, ot_cols], os.at[n], orc.at[n], partner)
        whole.wait_send()
        whole.wait_recv()
    for cp in tab:
        cp.wait()


def shards(
    queries, keys, values, out_grad, out_weight, time_gate, speaker_gate, time_steps, speakers, lengths
):
    any_spec = pl.BlockSpec(memory_space=pl.ANY)
    smem = pl.BlockSpec(memory_space=pltpu.SMEM)
    dma = pltpu.SemaphoreType.DMA
    vm = pltpu.VMEM
    out_rows = jax.ShapeDtypeStruct((ROWS, 2 * FEAT), BF)
    dq, dk, dv, tt, st = pl.pallas_call(
        kernel,
        name="attention_grads",
        out_shape=(
            out_rows, out_rows, out_rows,
            jax.ShapeDtypeStruct((TT, D), F32), jax.ShapeDtypeStruct((SPK, D), F32),
        ),
        in_specs=[smem] * 3 + [any_spec] * 7,
        out_specs=(any_spec,) * 5,
        scratch_shapes=[
            vm((2 * HALF, FEAT), BF), vm((2 * HALF, FEAT), BF), vm((2 * HALF, FEAT), BF),
            vm((2 * HALF, FEAT), BF),
            vm((HALF, D), BF), vm((HALF, D), BF), vm((FEAT, D), BF), vm((HALF, FEAT), BF),
            vm((HALF, FEAT), BF), vm((HALF, FEAT), BF), vm((HALF, FEAT), BF),
            vm((HALF, FEAT), F32), vm((HALF, FEAT), F32),
            vm((2, LOCAL_HEADS, 8, HALF), F32),
            vm((2, 8, 256), F32), vm((8, 256), F32), vm((8, 8, 256), F32),
            vm((4, 4, 4, 8, 256), F32),
            vm((TT, 2048), F32), vm((SPK, 2048), F32), vm((TT, D), F32), vm((SPK, D), F32),
            dma((8,)), dma((5,)), dma((5,)), dma((8,)), dma((4,)),
            dma((2, 4, 4)), dma((2, 4, 4)), dma((4, 8)), dma((4, 8)), dma((8,)), dma((8,)),
            dma((2,)), dma((8,)), dma((8,)), dma((2, 4)), dma((2, 4)),
            dma((5,)), dma((5,)), dma((5,)),
        ],
        compiler_params=pltpu.CompilerParams(
            collective_id=0, has_side_effects=True, vmem_limit_bytes=58 * 2**20
        ),
    )(
        time_steps, speakers, lengths,
        queries[0], keys[0], values[0], out_grad[0], out_weight, time_gate, speaker_gate,
    )
    return dq[None], dk[None], dv[None], tt, st


def solution(mesh):
    rows = P("fsdp", "seq", None)
    in_specs = (rows, rows, rows, rows, P("fsdp", "seq"), P(), P(), P(), P(), P())
    out_specs = (rows, rows, rows, P(), P())
    return jax.shard_map(shards, mesh=mesh, in_specs=in_specs, out_specs=out_specs, check_vma=False)
```

```python
import functools
import math

import jax
import jax.numpy as jnp
from jax import lax
from jax.experimental import pallas as pl
from jax.experimental.pallas import tpu as pltpu
from jax.sharding import PartitionSpec as P

HEAD_DIM = 128
LOCAL_HEADS = 8
HALF = 384
ROWS = 192
FEAT = 1024
D = 4096
TT = 32
SPK = 64
SCALE = HEAD_DIM ** (-0.5)
SCALE2 = SCALE / math.log(2.0)
MESH = pl.DeviceIdType.MESH
BF = jnp.bfloat16
F32 = jnp.float32

NT = (((1,), (1,)), ((), ()))
NN = (((1,), (0,)), ((), ()))
TN = (((0,), (0,)), ((), ()))


def dot(a, b, dims):
    return lax.dot_general(a, b, dims, preferred_element_type=F32)


def kernel(
    ts_ref, sp_ref, ln_ref,
    q_in, k_in, v_in, g_in, w_in, tg_in, sg_in,
    dq_out, dk_out, dv_out, tt_out, st_out,
    qb, kb, vb, db, gb, sb, wb, ob, dqv, dkv, dvv, dka, dva, stats,
    gp, gx, zb, gat, ttv, stv, tgv, sgv,
    loc, ps, pr, wzs, wzr, ws, wr, zs, zr, ds_s, ds_r, g1, gzs, gzr, gxs, gxr, ol, os, orc,
):
    fs = lax.axis_index("fsdp")
    sq = lax.axis_index("seq")
    x = lax.rem(fs, 4)
    y = lax.rem(lax.div(fs, 4), 4)
    zl = lax.div(fs, 16)
    zh = lax.div(sq, 2)
    c = lax.rem(sq, 2)
    z = zh * 4 + zl
    oc = 1 - c

    def dev(dz=0, dy=0, dx=0, fc=0):
        z2 = lax.rem(z + dz, 8)
        y2 = lax.rem(y + dy, 4)
        x2 = lax.rem(x + dx, 4)
        c2 = oc if fc else c
        return (lax.rem(z2, 4) * 16 + y2 * 4 + x2, lax.div(z2, 4) * 2 + c2)

    def remote(src, dst, ss, rs, to):
        return pltpu.make_async_remote_copy(
            src_ref=src, dst_ref=dst, send_sem=ss, recv_sem=rs, device_id=to, device_id_type=MESH
        )

    partner = dev(fc=1)
    anti = dev(dz=4)

    bar = pltpu.get_barrier_semaphore()
    peers = [partner]
    peers += [dev(dz=d) for d in range(1, 8)]
    peers += [dev(dx=d) for d in range(1, 4)]
    peers += [dev(dy=d) for d in range(1, 4)]
    for p in peers:
        pl.semaphore_signal(bar, inc=1, device_id=p, device_id_type=MESH)
    pl.semaphore_wait(bar, len(peers))

    my_rows = pl.ds(pl.multiple_of(c * ROWS, 64), ROWS)
    ot_rows = pl.ds(pl.multiple_of(oc * ROWS, 64), ROWS)
    my_cols = pl.ds(pl.multiple_of(c * FEAT, FEAT), FEAT)
    ot_cols = pl.ds(pl.multiple_of(oc * FEAT, FEAT), FEAT)

    ch = lax.div(zl, 2)
    wt = lax.rem(zl, 2)
    wrow = pl.ds(pl.multiple_of(wt * 512 + y * 128 + x * 32, 32), 32)
    wcol = pl.ds(pl.multiple_of(sq * 1024, 1024), 1024)
    w_own = pltpu.make_async_copy(w_in, wb.at[wrow, wcol], loc.at[4])
    w_pair = remote(w_in, wb.at[wrow, wcol], ps.at[4], pr.at[4], partner)
    pl.when(c == ch)(w_own.start)
    pl.when(c != ch)(w_pair.start)

    pair = []
    for n, (src, dst) in enumerate(((k_in, kb), (v_in, vb), (q_in, qb))):
        pair.append((
            pltpu.make_async_copy(src.at[:, my_cols], dst.at[my_rows, :], loc.at[n]),
            remote(src.at[:, ot_cols], dst.at[my_rows, :], ps.at[n], pr.at[n], partner),
            remote(src.at[:, ot_cols], dst.at[ot_rows, :], ps.at[n], pr.at[n], partner),
        ))
    pair.append((
        pltpu.make_async_copy(g_in, gb.at[my_rows, :], loc.at[3]),
        remote(g_in, gb.at[my_rows, :], ps.at[3], pr.at[3], partner),
        remote(g_in, gb.at[ot_rows, :], ps.at[3], pr.at[3], partner),
    ))
    for a, b, _ in pair:
        b.start()
        a.start()
    tg_copy = pltpu.make_async_copy(tg_in, tgv, loc.at[5])
    sg_copy = pltpu.make_async_copy(sg_in, sgv, loc.at[6])
    tg_copy.start()
    sg_copy.start()

    def head(j):
        return pl.ds(pl.multiple_of(j * HEAD_DIM, HEAD_DIM), HEAD_DIM)

    own = pl.ds(0, HALF)
    other = pl.ds(HALF, HALF)

    def zcopy(n, j):
        buf = (kb, vb, qb, db)[n]
        return remote(
            buf.at[own, head(j)], buf.at[other, head(j)], zs.at[n, j], zr.at[n, j], anti
        )

    def pair_wait(n):
        a, _, r = pair[n]
        a.wait()
        r.wait_recv()

    def wblock(t, h):
        return wb.at[
            pl.ds(pl.multiple_of(t * 512 + y * 128 + x * 32, 32), 32), pl.ds(h * 2048, 2048)
        ]

    wblocks = []
    for t in range(2):
        for h in range(2):
            wblocks.append((t, h, lax.rem(z + 16 - (4 * h + 2 * c + t), 8)))

    def wz(t, h, n, d):
        return remote(wblock(t, h), wblock(t, h), wzs.at[t * 2 + h, n], wzr.at[t * 2 + h], dev(dz=d))

    @pl.when(c == ch)
    def _():
        w_own.wait()
        remote(
            w_in, wb.at[wrow, pl.ds(pl.multiple_of((zh * 2 + oc) * 1024, 1024), 1024)],
            ps.at[4], pr.at[4], partner,
        ).wait_recv()

    def wz_start(t, h, hops):
        def go():
            for n, d in enumerate(hops):
                wz(t, h, n, d).start()
        return go

    def wz_sent(t, h, hops):
        def go():
            for n, d in enumerate(hops):
                wz(t, h, n, d).wait_send()
        return go

    def wz_pass(t, h, hops):
        def go():
            wz(t, h, 0, 1).wait_recv()
            wz_start(t, h, hops)()
        return go

    W0, W2, W6 = (2, 6), (1, 7, 2), (1, 7)
    for t, h, d in wblocks:
        pl.when(d == 0)(wz_start(t, h, W0))

    pair_wait(0)
    pair_wait(1)
    zcopy(0, 0).start()
    zcopy(1, 0).start()

    for t, h, d in wblocks:
        pl.when(d == 2)(wz_pass(t, h, W2))
        pl.when(d == 6)(wz_pass(t, h, W6))

    zcopy(0, 1).start()
    zcopy(1, 1).start()

    for t, h, d in wblocks:
        last = jnp.logical_or(lax.rem(d, 2) == 1, d == 4)
        pl.when(last)(wz(t, h, 0, 1).wait_recv)

    def unit(t, d1):
        if t == 0:
            r = y * 128 + lax.rem(x + 4 - d1, 4) * 32
        else:
            r = 512 + lax.rem(y + 4 - d1, 4) * 128 + x * 32
        return wb.at[pl.ds(pl.multiple_of(r, 32), 32), :]

    def axis_dev(axis, d):
        return dev(dx=d) if axis == 0 else dev(dy=d)

    def w1(t, d):
        return remote(unit(t, 0), unit(t, 0), ws.at[t, d, 0], wr.at[t, d, 0], axis_dev(t, d))

    def w2(t, d1, e):
        u = unit(t, d1)
        return remote(u, u, ws.at[t, d1, e], wr.at[t, d1, e], axis_dev(1 - t, e))

    for d in (1, 3, 2):
        for t in range(2):
            w1(t, d).start()
    for e in (1, 3, 2):
        for t in range(2):
            w2(t, 0, e).start()

    def w_forward():
        for d1 in (1, 3, 2):
            for t in range(2):
                u = unit(t, d1)
                remote(u, u, ws.at[t, d1, 0], wr.at[t, d1, 0], partner).wait_recv()
                for e in (1, 3, 2):
                    w2(t, d1, e).start()

    def w_finish():
        for d1 in range(4):
            for t in range(2):
                for e in range(1, 4):
                    if t == 0:
                        r = lax.rem(y + 4 - e, 4) * 128 + lax.rem(x + 4 - d1, 4) * 32
                    else:
                        r = 512 + lax.rem(y + 4 - d1, 4) * 128 + lax.rem(x + 4 - e, 4) * 32
                    u = wb.at[pl.ds(pl.multiple_of(r, 32), 32), :]
                    remote(u, u, ws.at[t, d1, e], wr.at[t, d1, e], partner).wait_recv()

    @pl.loop(2, LOCAL_HEADS)
    def _(j):
        zcopy(0, j).start()
        zcopy(1, j).start()

    pair_wait(2)

    @pl.loop(0, LOCAL_HEADS)
    def _(j):
        zcopy(2, j).start()

    tg_copy.wait()
    sg_copy.wait()
    gate = tgv[pl.ds(ts_ref[fs], 1), :] + sgv[pl.ds(sp_ref[fs], 1), :]
    pair_wait(3)
    for blk in range(8):
        cols = slice(blk * 512, (blk + 1) * 512)
        sb[:, cols] = (gb[:, cols].astype(F32) * gate[:, cols]).astype(BF)

    length = ln_ref[fs]
    key_pos = lax.broadcasted_iota(jnp.int32, (2 * HALF, 1), 0)
    frame = jnp.where(key_pos < HALF, zh * HALF + key_pos, (1 - zh) * HALF + key_pos - HALF)
    live = frame < length

    @pl.loop(0, LOCAL_HEADS)
    def _(j):
        pl.when(j == 1)(w_forward)
        zcopy(0, j).wait_recv()
        zcopy(1, j).wait_recv()
        s = dot(kb[:, head(j)], qb[own, head(j)], NT) * SCALE2
        s = jnp.where(live, s, -1e30)
        top = jnp.max(s, axis=0, keepdims=True)
        e = jnp.exp2(s - top)
        tot = jnp.sum(e, axis=0, keepdims=True)
        p = (e * (1.0 / tot)).astype(BF)
        ob[:, head(j)] = dot(p, vb[:, head(j)], TN).astype(BF)
        stats[0, 0, pl.ds(j, 1), :] = top + jnp.log2(tot)

    w_finish()

    @pl.loop(0, 16)
    def _(i):
        cols = pl.ds(pl.multiple_of(i * 256, 256), 256)
        proj = dot(ob[...], wb[:, cols], NN)
        part = jnp.sum(proj * gb[:, cols].astype(F32), axis=0, keepdims=True)
        gp[lax.div(i, 8), pl.ds(lax.rem(i, 8), 1), :] = part

    g1_copy = remote(gp.at[oc], gx, g1.at[0], g1.at[1], partner)
    g1_copy.start()

    gz_out = [remote(zb.at[z], zb.at[z], gzs.at[d], gzr.at[z], dev(dz=d)) for d in range(1, 8)]
    gx_src = gat.at[:, y, x]
    gx_out = [remote(gx_src, gx_src, gxs.at[0, d], gxr.at[0, d], dev(dx=d)) for d in range(1, 4)]
    gy_src = gat.at[:, y]
    gy_out = [remote(gy_src, gy_src, gxs.at[1, d], gxr.at[1, d], dev(dy=d)) for d in range(1, 4)]

    def gate_z():
        g1_copy.wait()
        zb[z] = gp[c] + gx[...]
        for cp in gz_out:
            cp.start()

    def gate_x():
        for d in range(1, 8):
            zz = lax.rem(z + d, 8)
            remote(zb.at[zz], zb.at[zz], gzs.at[d], gzr.at[zz], partner).wait_recv()
        for k in range(4):
            gat[k, y, x] = zb[k] + zb[k + 4]
        for cp in gx_out:
            cp.start()

    def gate_y():
        for d in range(1, 4):
            r = gat.at[:, y, lax.rem(x + 4 - d, 4)]
            remote(r, r, gxs.at[0, d], gxr.at[0, d], partner).wait_recv()
        for cp in gy_out:
            cp.start()

    my_tab = pl.ds(pl.multiple_of(c * 2048, 2048), 2048)
    tab = []
    for n, (src, dst) in enumerate(((ttv, tt_out), (stv, st_out))):
        tab.append(pltpu.make_async_copy(src, dst.at[:, my_tab], ol.at[3 + n]))
        tab.append(remote(src, dst.at[:, my_tab], os.at[3 + n], orc.at[3 + n], partner))

    def gate_tables():
        for d in range(1, 4):
            r = gat.at[:, lax.rem(y + 4 - d, 4)]
            remote(r, r, gxs.at[1, d], gxr.at[1, d], partner).wait_recv()
        tcol = jnp.concatenate([jnp.full((1, 1), ts_ref[k], jnp.int32) for k in range(64)], axis=1)
        scol = jnp.concatenate([jnp.full((1, 1), sp_ref[k], jnp.int32) for k in range(64)], axis=1)
        hot_t = (lax.broadcasted_iota(jnp.int32, (TT, 64), 0) == tcol).astype(F32)
        hot_s = (lax.broadcasted_iota(jnp.int32, (SPK, 64), 0) == scol).astype(F32)
        for r in range(8):
            rows = gat[:, :, :, r, :].reshape(64, 256)
            cols = slice(r * 256, (r + 1) * 256)
            for hot, dst in ((hot_t, ttv), (hot_s, stv)):
                dst[:, cols] = lax.dot_general(
                    hot, rows, NN, preferred_element_type=F32, precision=lax.Precision.HIGHEST
                )
        for cp in tab:
            cp.start()

    gate_z()
    ones = jnp.ones((8, HEAD_DIM), F32)

    @pl.loop(0, LOCAL_HEADS // 2)
    def _(i):
        two = pl.ds(pl.multiple_of(i * 256, 256), 256)
        db[own, two] = dot(sb[...], wb[two, :], NT).astype(BF)
        for k in range(2):
            j = 2 * i + k
            prod = db[own, head(j)].astype(F32) * ob[:, head(j)].astype(F32)
            delta = lax.dot_general(
                ones, prod, NT, preferred_element_type=F32, precision=lax.Precision.HIGHEST
            )
            stats[0, 1, pl.ds(j, 1), :] = delta[0:1, :]

    stat_copy = remote(stats.at[0], stats.at[1], ds_s.at[0], ds_r.at[0], anti)
    stat_copy.start()

    @pl.loop(0, LOCAL_HEADS)
    def _(j):
        zcopy(3, j).start()

    outs = ((dqv, dq_out), (dkv, dk_out), (dvv, dv_out))

    def out_copies(n, j):
        src, dst = outs[n]
        to = dst.at[:, pl.ds(pl.multiple_of(c * FEAT + j * HEAD_DIM, HEAD_DIM), HEAD_DIM)]
        return (
            pltpu.make_async_copy(src.at[my_rows, head(j)], to, ol.at[n]),
            remote(src.at[ot_rows, head(j)], to, os.at[n], orc.at[n], partner),
        )

    @pl.loop(0, LOCAL_HEADS)
    def _(j):
        q = qb[own, head(j)]
        k = kb[:, head(j)]
        do = db[own, head(j)]
        s = jnp.where(live, dot(k, q, NT) * SCALE2, -1e30)
        p = jnp.exp2(s - stats[0, 0, pl.ds(j, 1), :])
        dp = dot(vb[:, head(j)], do, NT)
        ds = (p * (dp - stats[0, 1, pl.ds(j, 1), :])).astype(BF)
        dqv[:, head(j)] = (dot(ds, k, TN) * SCALE).astype(BF)
        dka[:, head(j)] = dot(ds[:HALF], q, NN)
        dva[:, head(j)] = dot(p[:HALF].astype(BF), do, NN)
        for cp in out_copies(0, j):
            cp.start()

    gate_x()
    stat_copy.wait_recv()

    @pl.loop(0, LOCAL_HEADS)
    def _(j):
        pl.when(j == 1)(gate_y)
        pl.when(j == 3)(gate_tables)
        zcopy(2, j).wait_recv()
        zcopy(3, j).wait_recv()
        q = qb[other, head(j)]
        do = db[other, head(j)]
        s = jnp.where(live[:HALF], dot(kb[own, head(j)], q, NT) * SCALE2, -1e30)
        p = jnp.exp2(s - stats[1, 0, pl.ds(j, 1), :])
        dp = dot(vb[own, head(j)], do, NT)
        ds = (p * (dp - stats[1, 1, pl.ds(j, 1), :])).astype(BF)
        dkv[:, head(j)] = ((dka[:, head(j)] + dot(ds, q, NN)) * SCALE).astype(BF)
        dvv[:, head(j)] = (dva[:, head(j)] + dot(p.astype(BF), do, NN)).astype(BF)
        for n in (1, 2):
            for cp in out_copies(n, j):
                cp.start()

    for _, b, _ in pair:
        b.wait_send()
    pl.when(c != ch)(w_pair.wait_send)

    for t, h, d in wblocks:
        pl.when(d == 0)(wz_sent(t, h, W0))
        pl.when(d == 2)(wz_sent(t, h, W2))
        pl.when(d == 6)(wz_sent(t, h, W6))

    for t in range(2):
        for d in range(1, 4):
            w1(t, d).wait_send()
        for d1 in range(4):
            for e in range(1, 4):
                w2(t, d1, e).wait_send()

    @pl.loop(0, LOCAL_HEADS)
    def _(j):
        for n in range(4):
            zcopy(n, j).wait_send()

    for cp in [stat_copy] + gz_out + gx_out + gy_out:
        cp.wait_send()
    for n, (src, dst) in enumerate(outs):
        pltpu.make_async_copy(src.at[my_rows, :], dst.at[:, my_cols], ol.at[n]).wait()
        whole = remote(src.at[ot_rows, :], dst.at[:, ot_cols], os.at[n], orc.at[n], partner)
        whole.wait_send()
        whole.wait_recv()
    for cp in tab:
        cp.wait()


def shards(
    queries, keys, values, out_grad, out_weight, time_gate, speaker_gate, time_steps, speakers, lengths
):
    any_spec = pl.BlockSpec(memory_space=pl.ANY)
    smem = pl.BlockSpec(memory_space=pltpu.SMEM)
    dma = pltpu.SemaphoreType.DMA
    vm = pltpu.VMEM
    out_rows = jax.ShapeDtypeStruct((ROWS, 2 * FEAT), BF)
    dq, dk, dv, tt, st = pl.pallas_call(
        kernel,
        name="attention_grads",
        out_shape=(
            out_rows, out_rows, out_rows,
            jax.ShapeDtypeStruct((TT, D), F32), jax.ShapeDtypeStruct((SPK, D), F32),
        ),
        in_specs=[smem] * 3 + [any_spec] * 7,
        out_specs=(any_spec,) * 5,
        scratch_shapes=[
            vm((2 * HALF, FEAT), BF), vm((2 * HALF, FEAT), BF), vm((2 * HALF, FEAT), BF),
            vm((2 * HALF, FEAT), BF),
            vm((HALF, D), BF), vm((HALF, D), BF), vm((FEAT, D), BF), vm((HALF, FEAT), BF),
            vm((HALF, FEAT), BF), vm((HALF, FEAT), BF), vm((HALF, FEAT), BF),
            vm((HALF, FEAT), F32), vm((HALF, FEAT), F32),
            vm((2, 2, LOCAL_HEADS, HALF), F32),
            vm((2, 8, 256), F32), vm((8, 256), F32), vm((8, 8, 256), F32),
            vm((4, 4, 4, 8, 256), F32),
            vm((TT, 2048), F32), vm((SPK, 2048), F32), vm((TT, D), F32), vm((SPK, D), F32),
            dma((8,)), dma((5,)), dma((5,)), dma((4, 3)), dma((4,)),
            dma((2, 4, 4)), dma((2, 4, 4)), dma((4, 8)), dma((4, 8)), dma((1,)), dma((1,)),
            dma((2,)), dma((8,)), dma((8,)), dma((2, 4)), dma((2, 4)),
            dma((5,)), dma((5,)), dma((5,)),
        ],
        compiler_params=pltpu.CompilerParams(
            collective_id=0, has_side_effects=True, vmem_limit_bytes=58 * 2**20
        ),
    )(
        time_steps, speakers, lengths,
        queries[0], keys[0], values[0], out_grad[0], out_weight, time_gate, speaker_gate,
    )
    return dq[None], dk[None], dv[None], tt, st


def solution(mesh):
    rows = P("fsdp", "seq", None)
    in_specs = (rows, rows, rows, rows, P("fsdp", "seq"), P(), P(), P(), P(), P())
    out_specs = (rows, rows, rows, P(), P())
    return jax.shard_map(shards, mesh=mesh, in_specs=in_specs, out_specs=out_specs, check_vma=False)
```

```python
import functools
import math

import jax
import jax.numpy as jnp
from jax import lax
from jax.experimental import pallas as pl
from jax.experimental.pallas import tpu as pltpu
from jax.sharding import PartitionSpec as P

HEAD_DIM = 128
LOCAL_HEADS = 8
HALF = 384
ROWS = 192
FEAT = 1024
D = 4096
TT = 32
SPK = 64
SCALE = HEAD_DIM ** (-0.5)
SCALE2 = SCALE / math.log(2.0)
MESH = pl.DeviceIdType.MESH
BF = jnp.bfloat16
F32 = jnp.float32

NT = (((1,), (1,)), ((), ()))
NN = (((1,), (0,)), ((), ()))
TN = (((0,), (0,)), ((), ()))


def dot(a, b, dims):
    return lax.dot_general(a, b, dims, preferred_element_type=F32)


def kernel(
    ts_ref, sp_ref, ln_ref,
    q_in, k_in, v_in, g_in, w_in, tg_in, sg_in,
    dq_out, dk_out, dv_out, tt_out, st_out,
    qb, kb, vb, db, gb, sb, wb, ob, dqv, dkv, dvv, dka, dva, stats,
    gp, gx, zb, gat, ttv, stv, tgv, sgv,
    loc, ps, pr, wzs, wzr, ws, wsr, wr, zs, zr, ds_s, ds_r, g1, gzs, gzr, gxs, gxr, ol, os, orc,
):
    fs = lax.axis_index("fsdp")
    sq = lax.axis_index("seq")
    x = lax.rem(fs, 4)
    y = lax.rem(lax.div(fs, 4), 4)
    zl = lax.div(fs, 16)
    zh = lax.div(sq, 2)
    c = lax.rem(sq, 2)
    z = zh * 4 + zl
    oc = 1 - c

    def dev(dz=0, dy=0, dx=0, fc=0):
        z2 = lax.rem(z + dz, 8)
        y2 = lax.rem(y + dy, 4)
        x2 = lax.rem(x + dx, 4)
        c2 = oc if fc else c
        return (lax.rem(z2, 4) * 16 + y2 * 4 + x2, lax.div(z2, 4) * 2 + c2)

    def remote(src, dst, ss, rs, to):
        return pltpu.make_async_remote_copy(
            src_ref=src, dst_ref=dst, send_sem=ss, recv_sem=rs, device_id=to, device_id_type=MESH
        )

    partner = dev(fc=1)
    anti = dev(dz=4)

    bar = pltpu.get_barrier_semaphore()
    peers = [partner]
    peers += [dev(dz=d) for d in range(1, 8)]
    peers += [dev(dx=d) for d in range(1, 4)]
    peers += [dev(dy=d) for d in range(1, 4)]
    for p in peers:
        pl.semaphore_signal(bar, inc=1, device_id=p, device_id_type=MESH)
    pl.semaphore_wait(bar, len(peers))

    my_rows = pl.ds(pl.multiple_of(c * ROWS, 64), ROWS)
    ot_rows = pl.ds(pl.multiple_of(oc * ROWS, 64), ROWS)
    my_cols = pl.ds(pl.multiple_of(c * FEAT, FEAT), FEAT)
    ot_cols = pl.ds(pl.multiple_of(oc * FEAT, FEAT), FEAT)

    ch = lax.div(zl, 2)
    wt = lax.rem(zl, 2)
    wrow = pl.ds(pl.multiple_of(wt * 512 + y * 128 + x * 32, 32), 32)
    wcol = pl.ds(pl.multiple_of(sq * 1024, 1024), 1024)
    w_own = pltpu.make_async_copy(w_in, wb.at[wrow, wcol], loc.at[4])
    w_pair = remote(w_in, wb.at[wrow, wcol], ps.at[4], pr.at[4], partner)
    pl.when(c == ch)(w_own.start)
    pl.when(c != ch)(w_pair.start)

    pair = []
    for n, (src, dst) in enumerate(((k_in, kb), (v_in, vb), (q_in, qb))):
        pair.append((
            pltpu.make_async_copy(src.at[:, my_cols], dst.at[my_rows, :], loc.at[n]),
            remote(src.at[:, ot_cols], dst.at[my_rows, :], ps.at[n], pr.at[n], partner),
            remote(src.at[:, ot_cols], dst.at[ot_rows, :], ps.at[n], pr.at[n], partner),
        ))
    pair.append((
        pltpu.make_async_copy(g_in, gb.at[my_rows, :], loc.at[3]),
        remote(g_in, gb.at[my_rows, :], ps.at[3], pr.at[3], partner),
        remote(g_in, gb.at[ot_rows, :], ps.at[3], pr.at[3], partner),
    ))
    for a, b, _ in pair:
        b.start()
        a.start()
    tg_copy = pltpu.make_async_copy(tg_in, tgv, loc.at[5])
    sg_copy = pltpu.make_async_copy(sg_in, sgv, loc.at[6])
    tg_copy.start()
    sg_copy.start()

    def head(j):
        return pl.ds(pl.multiple_of(j * HEAD_DIM, HEAD_DIM), HEAD_DIM)

    own = pl.ds(0, HALF)
    other = pl.ds(HALF, HALF)

    def zcopy(n, j):
        buf = (kb, vb, qb, db)[n]
        return remote(
            buf.at[own, head(j)], buf.at[other, head(j)], zs.at[n, j], zr.at[n, j], anti
        )

    def pair_wait(n):
        a, _, r = pair[n]
        a.wait()
        r.wait_recv()

    def wblock(t, h):
        return wb.at[
            pl.ds(pl.multiple_of(t * 512 + y * 128 + x * 32, 32), 32), pl.ds(h * 2048, 2048)
        ]

    wblocks = []
    for t in range(2):
        for h in range(2):
            wblocks.append((t, h, lax.rem(z + 16 - (4 * h + 2 * c + t), 8)))

    def wz(t, h, n, d):
        return remote(wblock(t, h), wblock(t, h), wzs.at[t * 2 + h, n], wzr.at[t * 2 + h], dev(dz=d))

    @pl.when(c == ch)
    def _():
        w_own.wait()
        remote(
            w_in, wb.at[wrow, pl.ds(pl.multiple_of((zh * 2 + oc) * 1024, 1024), 1024)],
            ps.at[4], pr.at[4], partner,
        ).wait_recv()

    def wz_start(t, h, hops):
        def go():
            for n, d in enumerate(hops):
                wz(t, h, n, d).start()
        return go

    def wz_sent(t, h, hops):
        def go():
            for n, d in enumerate(hops):
                wz(t, h, n, d).wait_send()
        return go

    def wz_pass(t, h, hops):
        def go():
            wz(t, h, 0, 1).wait_recv()
            wz_start(t, h, hops)()
        return go

    W0, W2, W6 = (2, 6), (1, 7, 2), (1, 7)
    for t, h, d in wblocks:
        pl.when(d == 0)(wz_start(t, h, W0))

    pair_wait(0)
    pair_wait(1)
    zcopy(0, 0).start()
    zcopy(1, 0).start()

    for t, h, d in wblocks:
        pl.when(d == 2)(wz_pass(t, h, W2))
        pl.when(d == 6)(wz_pass(t, h, W6))

    zcopy(0, 1).start()
    zcopy(1, 1).start()

    for t, h, d in wblocks:
        last = jnp.logical_or(lax.rem(d, 2) == 1, d == 4)
        pl.when(last)(wz(t, h, 0, 1).wait_recv)

    def unit(t, d, e, half=None):
        if t == 0:
            r = lax.rem(y + 4 - e, 4) * 128 + lax.rem(x + 4 - d, 4) * 32
        else:
            r = 512 + lax.rem(y + 4 - d, 4) * 128 + lax.rem(x + 4 - e, 4) * 32
        if half is not None:
            return wb.at[pl.ds(pl.multiple_of(r + 16 * half, 16), 16), :]
        return wb.at[pl.ds(pl.multiple_of(r, 32), 32), :]

    def axis_dev(axis, d):
        return dev(dx=d) if axis == 0 else dev(dy=d)

    def w1(t, d):
        u = unit(t, 0, 0)
        return remote(u, u, ws.at[t, d, 0], wr.at[t, d, 0], axis_dev(t, d))

    def w2(t, d, e):
        u = unit(t, d, 0)
        return remote(u, u, ws.at[t, d, e], wr.at[t, d, e], axis_dev(1 - t, e))

    def w1_relay(t, d):
        u = unit(t, d, 0, (d - 1) // 2)
        return remote(u, u, wsr.at[t, 0, d], wr.at[t, 2, 0], axis_dev(t, d))

    def w2_relay(t, d, e):
        u = unit(t, d, e, (e - 1) // 2)
        return remote(u, u, wsr.at[t, 1 + d, e], wr.at[t, d, 2], axis_dev(1 - t, e))

    def w_wait(t, d, e):
        u = unit(t, d, e)
        remote(u, u, ws.at[t, d, e], wr.at[t, d, e], partner).wait_recv()

    near = (1, 3)
    for d in near:
        for t in range(2):
            w1(t, d).start()
    for e in near:
        for t in range(2):
            w2(t, 0, e).start()

    def w_stage0():
        for d in near:
            for t in range(2):
                w_wait(t, d, 0)
                w1_relay(t, d).start()
                for e in near:
                    w2(t, d, e).start()

    def w_stage1():
        for e in near:
            for t in range(2):
                w_wait(t, 0, e)
                w2_relay(t, 0, e).start()
        for t in range(2):
            w_wait(t, 2, 0)
            for e in near:
                w2(t, 2, e).start()

    def w_stage2():
        for d in near:
            for e in near:
                for t in range(2):
                    w_wait(t, d, e)
                    w2_relay(t, d, e).start()

    def w_stage3():
        for e in near:
            for t in range(2):
                w_wait(t, 2, e)
                w2_relay(t, 2, e).start()

    def w_finish():
        for d in range(4):
            for t in range(2):
                w_wait(t, d, 2)

    @pl.loop(2, LOCAL_HEADS)
    def _(j):
        zcopy(0, j).start()
        zcopy(1, j).start()

    pair_wait(2)

    @pl.loop(0, LOCAL_HEADS)
    def _(j):
        zcopy(2, j).start()

    tg_copy.wait()
    sg_copy.wait()
    gate = tgv[pl.ds(ts_ref[fs], 1), :] + sgv[pl.ds(sp_ref[fs], 1), :]
    pair_wait(3)
    for blk in range(8):
        cols = slice(blk * 512, (blk + 1) * 512)
        sb[:, cols] = (gb[:, cols].astype(F32) * gate[:, cols]).astype(BF)

    length = ln_ref[fs]
    key_pos = lax.broadcasted_iota(jnp.int32, (2 * HALF, 1), 0)
    frame = jnp.where(key_pos < HALF, zh * HALF + key_pos, (1 - zh) * HALF + key_pos - HALF)
    live = frame < length

    @pl.loop(0, LOCAL_HEADS)
    def _(j):
        for n, stage in enumerate((w_stage0, w_stage1, w_stage2, w_stage3)):
            pl.when(j == n)(stage)
        zcopy(0, j).wait_recv()
        zcopy(1, j).wait_recv()
        s = dot(kb[:, head(j)], qb[own, head(j)], NT) * SCALE2
        s = jnp.where(live, s, -1e30)
        top = jnp.max(s, axis=0, keepdims=True)
        e = jnp.exp2(s - top)
        tot = jnp.sum(e, axis=0, keepdims=True)
        p = (e * (1.0 / tot)).astype(BF)
        ob[:, head(j)] = dot(p, vb[:, head(j)], TN).astype(BF)
        stats[0, 0, pl.ds(j, 1), :] = top + jnp.log2(tot)

    w_finish()

    @pl.loop(0, 16)
    def _(i):
        cols = pl.ds(pl.multiple_of(i * 256, 256), 256)
        proj = dot(ob[...], wb[:, cols], NN)
        part = jnp.sum(proj * gb[:, cols].astype(F32), axis=0, keepdims=True)
        gp[lax.div(i, 8), pl.ds(lax.rem(i, 8), 1), :] = part

    g1_copy = remote(gp.at[oc], gx, g1.at[0], g1.at[1], partner)
    g1_copy.start()

    gz_out = [remote(zb.at[z], zb.at[z], gzs.at[d], gzr.at[z], dev(dz=d)) for d in range(1, 8)]
    gx_src = gat.at[:, y, x]
    gx_out = [remote(gx_src, gx_src, gxs.at[0, d], gxr.at[0, d], dev(dx=d)) for d in range(1, 4)]
    gy_src = gat.at[:, y]
    gy_out = [remote(gy_src, gy_src, gxs.at[1, d], gxr.at[1, d], dev(dy=d)) for d in range(1, 4)]

    def gate_z():
        g1_copy.wait()
        zb[z] = gp[c] + gx[...]
        for cp in gz_out:
            cp.start()

    def gate_x():
        for d in range(1, 8):
            zz = lax.rem(z + d, 8)
            remote(zb.at[zz], zb.at[zz], gzs.at[d], gzr.at[zz], partner).wait_recv()
        for k in range(4):
            gat[k, y, x] = zb[k] + zb[k + 4]
        for cp in gx_out:
            cp.start()

    def gate_y():
        for d in range(1, 4):
            r = gat.at[:, y, lax.rem(x + 4 - d, 4)]
            remote(r, r, gxs.at[0, d], gxr.at[0, d], partner).wait_recv()
        for cp in gy_out:
            cp.start()

    my_tab = pl.ds(pl.multiple_of(c * 2048, 2048), 2048)
    tab = []
    for n, (src, dst) in enumerate(((ttv, tt_out), (stv, st_out))):
        tab.append(pltpu.make_async_copy(src, dst.at[:, my_tab], ol.at[3 + n]))
        tab.append(remote(src, dst.at[:, my_tab], os.at[3 + n], orc.at[3 + n], partner))

    def gate_tables():
        for d in range(1, 4):
            r = gat.at[:, lax.rem(y + 4 - d, 4)]
            remote(r, r, gxs.at[1, d], gxr.at[1, d], partner).wait_recv()
        tcol = jnp.concatenate([jnp.full((1, 1), ts_ref[k], jnp.int32) for k in range(64)], axis=1)
        scol = jnp.concatenate([jnp.full((1, 1), sp_ref[k], jnp.int32) for k in range(64)], axis=1)
        hot_t = (lax.broadcasted_iota(jnp.int32, (TT, 64), 0) == tcol).astype(F32)
        hot_s = (lax.broadcasted_iota(jnp.int32, (SPK, 64), 0) == scol).astype(F32)
        for r in range(8):
            rows = gat[:, :, :, r, :].reshape(64, 256)
            cols = slice(r * 256, (r + 1) * 256)
            for hot, dst in ((hot_t, ttv), (hot_s, stv)):
                dst[:, cols] = lax.dot_general(
                    hot, rows, NN, preferred_element_type=F32, precision=lax.Precision.HIGHEST
                )
        for cp in tab:
            cp.start()

    gate_z()
    ones = jnp.ones((8, HEAD_DIM), F32)

    @pl.loop(0, LOCAL_HEADS // 2)
    def _(i):
        two = pl.ds(pl.multiple_of(i * 256, 256), 256)
        db[own, two] = dot(sb[...], wb[two, :], NT).astype(BF)
        for k in range(2):
            j = 2 * i + k
            prod = db[own, head(j)].astype(F32) * ob[:, head(j)].astype(F32)
            delta = lax.dot_general(
                ones, prod, NT, preferred_element_type=F32, precision=lax.Precision.HIGHEST
            )
            stats[0, 1, pl.ds(j, 1), :] = delta[0:1, :]

    stat_copy = remote(stats.at[0], stats.at[1], ds_s.at[0], ds_r.at[0], anti)
    stat_copy.start()

    @pl.loop(0, LOCAL_HEADS)
    def _(j):
        zcopy(3, j).start()

    outs = ((dqv, dq_out), (dkv, dk_out), (dvv, dv_out))

    def out_copies(n, j):
        src, dst = outs[n]
        to = dst.at[:, pl.ds(pl.multiple_of(c * FEAT + j * HEAD_DIM, HEAD_DIM), HEAD_DIM)]
        return (
            pltpu.make_async_copy(src.at[my_rows, head(j)], to, ol.at[n]),
            remote(src.at[ot_rows, head(j)], to, os.at[n], orc.at[n], partner),
        )

    @pl.loop(0, LOCAL_HEADS)
    def _(j):
        q = qb[own, head(j)]
        k = kb[:, head(j)]
        do = db[own, head(j)]
        s = jnp.where(live, dot(k, q, NT) * SCALE2, -1e30)
        p = jnp.exp2(s - stats[0, 0, pl.ds(j, 1), :])
        dp = dot(vb[:, head(j)], do, NT)
        ds = (p * (dp - stats[0, 1, pl.ds(j, 1), :])).astype(BF)
        dqv[:, head(j)] = (dot(ds, k, TN) * SCALE).astype(BF)
        dka[:, head(j)] = dot(ds[:HALF], q, NN)
        dva[:, head(j)] = dot(p[:HALF].astype(BF), do, NN)
        for cp in out_copies(0, j):
            cp.start()

    stat_copy.wait_recv()

    @pl.loop(0, LOCAL_HEADS)
    def _(j):
        pl.when(j == 2)(gate_x)
        pl.when(j == 4)(gate_y)
        pl.when(j == 6)(gate_tables)
        zcopy(2, j).wait_recv()
        zcopy(3, j).wait_recv()
        q = qb[other, head(j)]
        do = db[other, head(j)]
        s = jnp.where(live[:HALF], dot(kb[own, head(j)], q, NT) * SCALE2, -1e30)
        p = jnp.exp2(s - stats[1, 0, pl.ds(j, 1), :])
        dp = dot(vb[own, head(j)], do, NT)
        ds = (p * (dp - stats[1, 1, pl.ds(j, 1), :])).astype(BF)
        dkv[:, head(j)] = ((dka[:, head(j)] + dot(ds, q, NN)) * SCALE).astype(BF)
        dvv[:, head(j)] = (dva[:, head(j)] + dot(p.astype(BF), do, NN)).astype(BF)
        for n in (1, 2):
            for cp in out_copies(n, j):
                cp.start()

    for _, b, _ in pair:
        b.wait_send()
    pl.when(c != ch)(w_pair.wait_send)

    for t, h, d in wblocks:
        pl.when(d == 0)(wz_sent(t, h, W0))
        pl.when(d == 2)(wz_sent(t, h, W2))
        pl.when(d == 6)(wz_sent(t, h, W6))

    for t in range(2):
        for d in near:
            w1(t, d).wait_send()
            w1_relay(t, d).wait_send()
        for d in range(4):
            for e in near:
                w2(t, d, e).wait_send()
                w2_relay(t, d, e).wait_send()

    @pl.loop(0, LOCAL_HEADS)
    def _(j):
        for n in range(4):
            zcopy(n, j).wait_send()

    for cp in [stat_copy] + gz_out + gx_out + gy_out:
        cp.wait_send()
    for n, (src, dst) in enumerate(outs):
        pltpu.make_async_copy(src.at[my_rows, :], dst.at[:, my_cols], ol.at[n]).wait()
        whole = remote(src.at[ot_rows, :], dst.at[:, ot_cols], os.at[n], orc.at[n], partner)
        whole.wait_send()
        whole.wait_recv()
    for cp in tab:
        cp.wait()


def shards(
    queries, keys, values, out_grad, out_weight, time_gate, speaker_gate, time_steps, speakers, lengths
):
    any_spec = pl.BlockSpec(memory_space=pl.ANY)
    smem = pl.BlockSpec(memory_space=pltpu.SMEM)
    dma = pltpu.SemaphoreType.DMA
    vm = pltpu.VMEM
    out_rows = jax.ShapeDtypeStruct((ROWS, 2 * FEAT), BF)
    dq, dk, dv, tt, st = pl.pallas_call(
        kernel,
        name="attention_grads",
        out_shape=(
            out_rows, out_rows, out_rows,
            jax.ShapeDtypeStruct((TT, D), F32), jax.ShapeDtypeStruct((SPK, D), F32),
        ),
        in_specs=[smem] * 3 + [any_spec] * 7,
        out_specs=(any_spec,) * 5,
        scratch_shapes=[
            vm((2 * HALF, FEAT), BF), vm((2 * HALF, FEAT), BF), vm((2 * HALF, FEAT), BF),
            vm((2 * HALF, FEAT), BF),
            vm((HALF, D), BF), vm((HALF, D), BF), vm((FEAT, D), BF), vm((HALF, FEAT), BF),
            vm((HALF, FEAT), BF), vm((HALF, FEAT), BF), vm((HALF, FEAT), BF),
            vm((HALF, FEAT), F32), vm((HALF, FEAT), F32),
            vm((2, 2, LOCAL_HEADS, HALF), F32),
            vm((2, 8, 256), F32), vm((8, 256), F32), vm((8, 8, 256), F32),
            vm((4, 4, 4, 8, 256), F32),
            vm((TT, 2048), F32), vm((SPK, 2048), F32), vm((TT, D), F32), vm((SPK, D), F32),
            dma((8,)), dma((5,)), dma((5,)), dma((4, 3)), dma((4,)),
            dma((2, 4, 4)), dma((2, 5, 4)), dma((2, 4, 4)), dma((4, 8)), dma((4, 8)), dma((1,)), dma((1,)),
            dma((2,)), dma((8,)), dma((8,)), dma((2, 4)), dma((2, 4)),
            dma((5,)), dma((5,)), dma((5,)),
        ],
        compiler_params=pltpu.CompilerParams(
            collective_id=0, has_side_effects=True, vmem_limit_bytes=58 * 2**20
        ),
    )(
        time_steps, speakers, lengths,
        queries[0], keys[0], values[0], out_grad[0], out_weight, time_gate, speaker_gate,
    )
    return dq[None], dk[None], dv[None], tt, st


def solution(mesh):
    rows = P("fsdp", "seq", None)
    in_specs = (rows, rows, rows, rows, P("fsdp", "seq"), P(), P(), P(), P(), P())
    out_specs = (rows, rows, rows, P(), P())
    return jax.shard_map(shards, mesh=mesh, in_specs=in_specs, out_specs=out_specs, check_vma=False)
```

```python
import functools
import math

import jax
import jax.numpy as jnp
from jax import lax
from jax.experimental import pallas as pl
from jax.experimental.pallas import tpu as pltpu
from jax.sharding import PartitionSpec as P

HEAD_DIM = 128
LOCAL_HEADS = 8
HALF = 384
ROWS = 192
FEAT = 1024
D = 4096
TT = 32
SPK = 64
SCALE = HEAD_DIM ** (-0.5)
SCALE2 = SCALE / math.log(2.0)
MESH = pl.DeviceIdType.MESH
BF = jnp.bfloat16
F32 = jnp.float32

NT = (((1,), (1,)), ((), ()))
NN = (((1,), (0,)), ((), ()))
TN = (((0,), (0,)), ((), ()))


def dot(a, b, dims):
    return lax.dot_general(a, b, dims, preferred_element_type=F32)


def kernel(
    ts_ref, sp_ref, ln_ref,
    q_in, k_in, v_in, g_in, w_in, tg_in, sg_in,
    dq_out, dk_out, dv_out, tt_out, st_out,
    qb, kb, vb, db, gb, sb, wb, ob, dqv, dkv, dvv, dka, dva, stats,
    gp, gx, zb, gat, ttv, stv, tgv, sgv,
    loc, ps, pr, wzs, wzr, ws, wsr, wr, zs, zr, ds_s, ds_r, g1, gzs, gzr, gxs, gxr, ol, os, orc,
):
    fs = lax.axis_index("fsdp")
    sq = lax.axis_index("seq")
    x = lax.rem(fs, 4)
    y = lax.rem(lax.div(fs, 4), 4)
    zl = lax.div(fs, 16)
    zh = lax.div(sq, 2)
    c = lax.rem(sq, 2)
    z = zh * 4 + zl
    oc = 1 - c

    def dev(dz=0, dy=0, dx=0, fc=0):
        z2 = lax.rem(z + dz, 8)
        y2 = lax.rem(y + dy, 4)
        x2 = lax.rem(x + dx, 4)
        c2 = oc if fc else c
        return (lax.rem(z2, 4) * 16 + y2 * 4 + x2, lax.div(z2, 4) * 2 + c2)

    def remote(src, dst, ss, rs, to):
        return pltpu.make_async_remote_copy(
            src_ref=src, dst_ref=dst, send_sem=ss, recv_sem=rs, device_id=to, device_id_type=MESH
        )

    partner = dev(fc=1)
    anti = dev(dz=4)

    bar = pltpu.get_barrier_semaphore()
    peers = [partner]
    peers += [dev(dz=d) for d in range(1, 8)]
    peers += [dev(dx=d) for d in range(1, 4)]
    peers += [dev(dy=d) for d in range(1, 4)]
    for p in peers:
        pl.semaphore_signal(bar, inc=1, device_id=p, device_id_type=MESH)
    pl.semaphore_wait(bar, len(peers))

    my_rows = pl.ds(pl.multiple_of(c * ROWS, 64), ROWS)
    ot_rows = pl.ds(pl.multiple_of(oc * ROWS, 64), ROWS)
    my_cols = pl.ds(pl.multiple_of(c * FEAT, FEAT), FEAT)
    ot_cols = pl.ds(pl.multiple_of(oc * FEAT, FEAT), FEAT)

    ch = lax.div(zl, 2)
    wt = lax.rem(zl, 2)
    wrow = pl.ds(pl.multiple_of(wt * 512 + y * 128 + x * 32, 32), 32)
    wcol = pl.ds(pl.multiple_of(sq * 1024, 1024), 1024)
    w_own = pltpu.make_async_copy(w_in, wb.at[wrow, wcol], loc.at[4])
    w_pair = remote(w_in, wb.at[wrow, wcol], ps.at[4], pr.at[4], partner)
    pl.when(c == ch)(w_own.start)
    pl.when(c != ch)(w_pair.start)

    pair = []
    for n, (src, dst) in enumerate(((k_in, kb), (v_in, vb), (q_in, qb))):
        pair.append((
            pltpu.make_async_copy(src.at[:, my_cols], dst.at[my_rows, :], loc.at[n]),
            remote(src.at[:, ot_cols], dst.at[my_rows, :], ps.at[n], pr.at[n], partner),
            remote(src.at[:, ot_cols], dst.at[ot_rows, :], ps.at[n], pr.at[n], partner),
        ))
    pair.append((
        pltpu.make_async_copy(g_in, gb.at[my_rows, :], loc.at[3]),
        remote(g_in, gb.at[my_rows, :], ps.at[3], pr.at[3], partner),
        remote(g_in, gb.at[ot_rows, :], ps.at[3], pr.at[3], partner),
    ))
    for a, b, _ in pair:
        b.start()
        a.start()
    tg_copy = pltpu.make_async_copy(tg_in, tgv, loc.at[5])
    sg_copy = pltpu.make_async_copy(sg_in, sgv, loc.at[6])
    tg_copy.start()
    sg_copy.start()

    def head(j):
        return pl.ds(pl.multiple_of(j * HEAD_DIM, HEAD_DIM), HEAD_DIM)

    own = pl.ds(0, HALF)
    other = pl.ds(HALF, HALF)

    def zcopy(n, j):
        buf = (kb, vb, qb, db)[n]
        return remote(
            buf.at[own, head(j)], buf.at[other, head(j)], zs.at[n, j], zr.at[n, j], anti
        )

    def pair_wait(n):
        a, _, r = pair[n]
        a.wait()
        r.wait_recv()

    def wblock(t, h):
        return wb.at[
            pl.ds(pl.multiple_of(t * 512 + y * 128 + x * 32, 32), 32), pl.ds(h * 2048, 2048)
        ]

    wblocks = []
    for t in range(2):
        for h in range(2):
            wblocks.append((t, h, lax.rem(z + 16 - (4 * h + 2 * c + t), 8)))

    def wz(t, h, n, d):
        return remote(wblock(t, h), wblock(t, h), wzs.at[t * 2 + h, n], wzr.at[t * 2 + h], dev(dz=d))

    @pl.when(c == ch)
    def _():
        w_own.wait()
        remote(
            w_in, wb.at[wrow, pl.ds(pl.multiple_of((zh * 2 + oc) * 1024, 1024), 1024)],
            ps.at[4], pr.at[4], partner,
        ).wait_recv()

    def wz_start(t, h, hops):
        def go():
            for n, d in enumerate(hops):
                wz(t, h, n, d).start()
        return go

    def wz_sent(t, h, hops):
        def go():
            for n, d in enumerate(hops):
                wz(t, h, n, d).wait_send()
        return go

    def wz_pass(t, h, hops):
        def go():
            wz(t, h, 0, 1).wait_recv()
            wz_start(t, h, hops)()
        return go

    W0, W2, W6 = (2, 6), (1, 7, 2), (1, 7)
    for t, h, d in wblocks:
        pl.when(d == 0)(wz_start(t, h, W0))

    pair_wait(0)
    pair_wait(1)
    zcopy(0, 0).start()
    zcopy(1, 0).start()

    for t, h, d in wblocks:
        pl.when(d == 2)(wz_pass(t, h, W2))
        pl.when(d == 6)(wz_pass(t, h, W6))

    zcopy(0, 1).start()
    zcopy(1, 1).start()

    for t, h, d in wblocks:
        last = jnp.logical_or(lax.rem(d, 2) == 1, d == 4)
        pl.when(last)(wz(t, h, 0, 1).wait_recv)

    def unit(t, d, e, half=None):
        if t == 0:
            r = lax.rem(y + 4 - e, 4) * 128 + lax.rem(x + 4 - d, 4) * 32
        else:
            r = 512 + lax.rem(y + 4 - d, 4) * 128 + lax.rem(x + 4 - e, 4) * 32
        if half is not None:
            return wb.at[pl.ds(pl.multiple_of(r + 16 * half, 16), 16), :]
        return wb.at[pl.ds(pl.multiple_of(r, 32), 32), :]

    def axis_dev(axis, d):
        return dev(dx=d) if axis == 0 else dev(dy=d)

    def w1(t, d):
        u = unit(t, 0, 0)
        return remote(u, u, ws.at[t, d, 0], wr.at[t, d, 0], axis_dev(t, d))

    def w2(t, d, e):
        u = unit(t, d, 0)
        return remote(u, u, ws.at[t, d, e], wr.at[t, d, e], axis_dev(1 - t, e))

    def w1_relay(t, d):
        u = unit(t, d, 0, (d - 1) // 2)
        return remote(u, u, wsr.at[t, 0, d], wr.at[t, 2, 0], axis_dev(t, d))

    def w2_relay(t, d, e):
        u = unit(t, d, e, (e - 1) // 2)
        return remote(u, u, wsr.at[t, 1 + d, e], wr.at[t, d, 2], axis_dev(1 - t, e))

    def w_wait(t, d, e):
        u = unit(t, d, e)
        remote(u, u, ws.at[t, d, e], wr.at[t, d, e], partner).wait_recv()

    near = (1, 3)
    for d in near:
        for t in range(2):
            w1(t, d).start()
    for e in near:
        for t in range(2):
            w2(t, 0, e).start()

    def w_stage0():
        for d in near:
            for t in range(2):
                w_wait(t, d, 0)
                w1_relay(t, d).start()
                for e in near:
                    w2(t, d, e).start()

    def w_stage1():
        for e in near:
            for t in range(2):
                w_wait(t, 0, e)
                w2_relay(t, 0, e).start()
        for t in range(2):
            w_wait(t, 2, 0)
            for e in near:
                w2(t, 2, e).start()

    def w_stage2():
        for d in near:
            for e in near:
                for t in range(2):
                    w_wait(t, d, e)
                    w2_relay(t, d, e).start()

    def w_stage3():
        for e in near:
            for t in range(2):
                w_wait(t, 2, e)
                w2_relay(t, 2, e).start()

    def w_finish():
        for d in range(4):
            for t in range(2):
                w_wait(t, d, 2)

    @pl.loop(2, LOCAL_HEADS)
    def _(j):
        zcopy(0, j).start()
        zcopy(1, j).start()

    pair_wait(2)

    @pl.loop(0, 3)
    def _(j):
        zcopy(2, j).start()

    tg_copy.wait()
    sg_copy.wait()
    gate = tgv[pl.ds(ts_ref[fs], 1), :] + sgv[pl.ds(sp_ref[fs], 1), :]
    pair_wait(3)
    for blk in range(8):
        cols = slice(blk * 512, (blk + 1) * 512)
        sb[:, cols] = (gb[:, cols].astype(F32) * gate[:, cols]).astype(BF)

    length = ln_ref[fs]
    key_pos = lax.broadcasted_iota(jnp.int32, (2 * HALF, 1), 0)
    frame = jnp.where(key_pos < HALF, zh * HALF + key_pos, (1 - zh) * HALF + key_pos - HALF)
    live = frame < length

    @pl.loop(0, LOCAL_HEADS)
    def _(j):
        for n, stage in enumerate((w_stage0, w_stage1, w_stage2, w_stage3)):
            pl.when(j == n)(stage)
        zcopy(0, j).wait_recv()
        zcopy(1, j).wait_recv()
        s = dot(kb[:, head(j)], qb[own, head(j)], NT) * SCALE2
        s = jnp.where(live, s, -1e30)
        top = jnp.max(s, axis=0, keepdims=True)
        e = jnp.exp2(s - top)
        tot = jnp.sum(e, axis=0, keepdims=True)
        p = (e * (1.0 / tot)).astype(BF)
        ob[:, head(j)] = dot(p, vb[:, head(j)], TN).astype(BF)
        stats[0, 0, pl.ds(j, 1), :] = top + jnp.log2(tot)

    w_finish()

    @pl.loop(0, 16)
    def _(i):
        cols = pl.ds(pl.multiple_of(i * 256, 256), 256)
        proj = dot(ob[...], wb[:, cols], NN)
        part = jnp.sum(proj * gb[:, cols].astype(F32), axis=0, keepdims=True)
        gp[lax.div(i, 8), pl.ds(lax.rem(i, 8), 1), :] = part

    g1_copy = remote(gp.at[oc], gx, g1.at[0], g1.at[1], partner)
    g1_copy.start()

    gz_out = [remote(zb.at[z], zb.at[z], gzs.at[d], gzr.at[z], dev(dz=d)) for d in range(1, 8)]
    gx_src = gat.at[:, y, x]
    gx_out = [remote(gx_src, gx_src, gxs.at[0, d], gxr.at[0, d], dev(dx=d)) for d in range(1, 4)]
    gy_src = gat.at[:, y]
    gy_out = [remote(gy_src, gy_src, gxs.at[1, d], gxr.at[1, d], dev(dy=d)) for d in range(1, 4)]

    def gate_z():
        g1_copy.wait()
        zb[z] = gp[c] + gx[...]
        for cp in gz_out:
            cp.start()

    def gate_x():
        for d in range(1, 8):
            zz = lax.rem(z + d, 8)
            remote(zb.at[zz], zb.at[zz], gzs.at[d], gzr.at[zz], partner).wait_recv()
        for k in range(4):
            gat[k, y, x] = zb[k] + zb[k + 4]
        for cp in gx_out:
            cp.start()

    def gate_y():
        for d in range(1, 4):
            r = gat.at[:, y, lax.rem(x + 4 - d, 4)]
            remote(r, r, gxs.at[0, d], gxr.at[0, d], partner).wait_recv()
        for cp in gy_out:
            cp.start()

    my_tab = pl.ds(pl.multiple_of(c * 2048, 2048), 2048)
    tab = []
    for n, (src, dst) in enumerate(((ttv, tt_out), (stv, st_out))):
        tab.append(pltpu.make_async_copy(src, dst.at[:, my_tab], ol.at[3 + n]))
        tab.append(remote(src, dst.at[:, my_tab], os.at[3 + n], orc.at[3 + n], partner))

    def gate_tables():
        for d in range(1, 4):
            r = gat.at[:, lax.rem(y + 4 - d, 4)]
            remote(r, r, gxs.at[1, d], gxr.at[1, d], partner).wait_recv()
        tcol = jnp.concatenate([jnp.full((1, 1), ts_ref[k], jnp.int32) for k in range(64)], axis=1)
        scol = jnp.concatenate([jnp.full((1, 1), sp_ref[k], jnp.int32) for k in range(64)], axis=1)
        hot_t = (lax.broadcasted_iota(jnp.int32, (TT, 64), 0) == tcol).astype(F32)
        hot_s = (lax.broadcasted_iota(jnp.int32, (SPK, 64), 0) == scol).astype(F32)
        for r in range(8):
            rows = gat[:, :, :, r, :].reshape(64, 256)
            cols = slice(r * 256, (r + 1) * 256)
            for hot, dst in ((hot_t, ttv), (hot_s, stv)):
                dst[:, cols] = lax.dot_general(
                    hot, rows, NN, preferred_element_type=F32, precision=lax.Precision.HIGHEST
                )
        for cp in tab:
            cp.start()

    ones = jnp.ones((8, HEAD_DIM), F32)

    @pl.loop(0, LOCAL_HEADS // 2)
    def _(i):
        two = pl.ds(pl.multiple_of(i * 256, 256), 256)
        db[own, two] = dot(sb[...], wb[two, :], NT).astype(BF)
        for k in range(2):
            j = 2 * i + k
            prod = db[own, head(j)].astype(F32) * ob[:, head(j)].astype(F32)
            delta = lax.dot_general(
                ones, prod, NT, preferred_element_type=F32, precision=lax.Precision.HIGHEST
            )
            stats[0, 1, pl.ds(j, 1), :] = delta[0:1, :]

    gate_z()
    gate_x()

    @pl.loop(3, LOCAL_HEADS)
    def _(j):
        zcopy(2, j).start()

    stat_copy = remote(stats.at[0], stats.at[1], ds_s.at[0], ds_r.at[0], anti)
    stat_copy.start()

    @pl.loop(0, LOCAL_HEADS)
    def _(j):
        zcopy(3, j).start()

    outs = ((dqv, dq_out), (dkv, dk_out), (dvv, dv_out))

    def out_copies(n, j):
        src, dst = outs[n]
        to = dst.at[:, pl.ds(pl.multiple_of(c * FEAT + j * HEAD_DIM, HEAD_DIM), HEAD_DIM)]
        return (
            pltpu.make_async_copy(src.at[my_rows, head(j)], to, ol.at[n]),
            remote(src.at[ot_rows, head(j)], to, os.at[n], orc.at[n], partner),
        )

    @pl.loop(0, LOCAL_HEADS)
    def _(j):
        q = qb[own, head(j)]
        k = kb[:, head(j)]
        do = db[own, head(j)]
        s = jnp.where(live, dot(k, q, NT) * SCALE2, -1e30)
        p = jnp.exp2(s - stats[0, 0, pl.ds(j, 1), :])
        dp = dot(vb[:, head(j)], do, NT)
        ds = (p * (dp - stats[0, 1, pl.ds(j, 1), :])).astype(BF)
        dqv[:, head(j)] = (dot(ds, k, TN) * SCALE).astype(BF)
        dka[:, head(j)] = dot(ds[:HALF], q, NN)
        dva[:, head(j)] = dot(p[:HALF].astype(BF), do, NN)
        for cp in out_copies(0, j):
            cp.start()
        pl.when(j == 1)(gate_y)
        pl.when(j == 4)(gate_tables)

    stat_copy.wait_recv()

    @pl.loop(0, LOCAL_HEADS)
    def _(j):
        zcopy(2, j).wait_recv()
        zcopy(3, j).wait_recv()
        q = qb[other, head(j)]
        do = db[other, head(j)]
        s = jnp.where(live[:HALF], dot(kb[own, head(j)], q, NT) * SCALE2, -1e30)
        p = jnp.exp2(s - stats[1, 0, pl.ds(j, 1), :])
        dp = dot(vb[own, head(j)], do, NT)
        ds = (p * (dp - stats[1, 1, pl.ds(j, 1), :])).astype(BF)
        dkv[:, head(j)] = ((dka[:, head(j)] + dot(ds, q, NN)) * SCALE).astype(BF)
        dvv[:, head(j)] = (dva[:, head(j)] + dot(p.astype(BF), do, NN)).astype(BF)
        for n in (1, 2):
            for cp in out_copies(n, j):
                cp.start()

    for _, b, _ in pair:
        b.wait_send()
    pl.when(c != ch)(w_pair.wait_send)

    for t, h, d in wblocks:
        pl.when(d == 0)(wz_sent(t, h, W0))
        pl.when(d == 2)(wz_sent(t, h, W2))
        pl.when(d == 6)(wz_sent(t, h, W6))

    for t in range(2):
        for d in near:
            w1(t, d).wait_send()
            w1_relay(t, d).wait_send()
        for d in range(4):
            for e in near:
                w2(t, d, e).wait_send()
                w2_relay(t, d, e).wait_send()

    @pl.loop(0, LOCAL_HEADS)
    def _(j):
        for n in range(4):
            zcopy(n, j).wait_send()

    for cp in [stat_copy] + gz_out + gx_out + gy_out:
        cp.wait_send()
    for n, (src, dst) in enumerate(outs):
        pltpu.make_async_copy(src.at[my_rows, :], dst.at[:, my_cols], ol.at[n]).wait()
        whole = remote(src.at[ot_rows, :], dst.at[:, ot_cols], os.at[n], orc.at[n], partner)
        whole.wait_send()
        whole.wait_recv()
    for cp in tab:
        cp.wait()


def shards(
    queries, keys, values, out_grad, out_weight, time_gate, speaker_gate, time_steps, speakers, lengths
):
    any_spec = pl.BlockSpec(memory_space=pl.ANY)
    smem = pl.BlockSpec(memory_space=pltpu.SMEM)
    dma = pltpu.SemaphoreType.DMA
    vm = pltpu.VMEM
    out_rows = jax.ShapeDtypeStruct((ROWS, 2 * FEAT), BF)
    dq, dk, dv, tt, st = pl.pallas_call(
        kernel,
        name="attention_grads",
        out_shape=(
            out_rows, out_rows, out_rows,
            jax.ShapeDtypeStruct((TT, D), F32), jax.ShapeDtypeStruct((SPK, D), F32),
        ),
        in_specs=[smem] * 3 + [any_spec] * 7,
        out_specs=(any_spec,) * 5,
        scratch_shapes=[
            vm((2 * HALF, FEAT), BF), vm((2 * HALF, FEAT), BF), vm((2 * HALF, FEAT), BF),
            vm((2 * HALF, FEAT), BF),
            vm((HALF, D), BF), vm((HALF, D), BF), vm((FEAT, D), BF), vm((HALF, FEAT), BF),
            vm((HALF, FEAT), BF), vm((HALF, FEAT), BF), vm((HALF, FEAT), BF),
            vm((HALF, FEAT), F32), vm((HALF, FEAT), F32),
            vm((2, 2, LOCAL_HEADS, HALF), F32),
            vm((2, 8, 256), F32), vm((8, 256), F32), vm((8, 8, 256), F32),
            vm((4, 4, 4, 8, 256), F32),
            vm((TT, 2048), F32), vm((SPK, 2048), F32), vm((TT, D), F32), vm((SPK, D), F32),
            dma((8,)), dma((5,)), dma((5,)), dma((4, 3)), dma((4,)),
            dma((2, 4, 4)), dma((2, 5, 4)), dma((2, 4, 4)), dma((4, 8)), dma((4, 8)), dma((1,)), dma((1,)),
            dma((2,)), dma((8,)), dma((8,)), dma((2, 4)), dma((2, 4)),
            dma((5,)), dma((5,)), dma((5,)),
        ],
        compiler_params=pltpu.CompilerParams(
            collective_id=0, has_side_effects=True, vmem_limit_bytes=58 * 2**20
        ),
    )(
        time_steps, speakers, lengths,
        queries[0], keys[0], values[0], out_grad[0], out_weight, time_gate, speaker_gate,
    )
    return dq[None], dk[None], dv[None], tt, st


def solution(mesh):
    rows = P("fsdp", "seq", None)
    in_specs = (rows, rows, rows, rows, P("fsdp", "seq"), P(), P(), P(), P(), P())
    out_specs = (rows, rows, rows, P(), P())
    return jax.shard_map(shards, mesh=mesh, in_specs=in_specs, out_specs=out_specs, check_vma=False)
```
